512 devices in a mesh: row: 32 (over y, x), col: 16 (over z, core).
Axes of the slice: x: 4, y: 8, z: 8, core: 2. Of those that a mesh axis runs over, the one named last changes fastest.
Arguments:
- panel: float32 [2, 8192, 256], P(None, 'row', 'col'), may hold values from -100 to 100
- matrix: float32 [2, 8192, 4, 4096], P(None, 'row', None, 'col'), may hold values from -85 to 85, as said below
Outputs:
- updated: float32 [2, 8192, 4, 4096], P(None, 'row', None, 'col')
- r_factor: float32 [256, 256], replicated
The draws below stay inside these ranges and needn't reach their ends.
Inputs may be any that keep to these rules, and one draw needn't show every extreme that they name: matrix, read as in the reference program, is symmetric.
All inputs are finite; a program needn't handle non-finite values.
Results may differ from the reference program's by a relative error of at most 0.000092.
Values sent between devices are 32-bit elements; how exact they have to be, the bound alone decides.
A program may use at most 64 MiB of HBM per device.

```python
import jax
import jax.numpy as jnp
from jax import lax

N = 16384
NB = 256
CYC_R = 2
CYC_C = 4


def draw_panel(key, part):
    key = jax.random.fold_in(key, 11)
    key_base, key_scale, key_gain, key_top, key_common, key_mixing = jax.random.split(key, 6)
    below_rows = N - NB
    base = jnp.clip(jax.random.normal(key_base, (below_rows, NB), jnp.float32), -6.0, 6.0)
    common = jnp.clip(jax.random.normal(key_common, (below_rows, 8), jnp.float32), -6.0, 6.0)
    scales = jnp.exp(jax.random.uniform(key_scale, (below_rows, 1), jnp.float32, 0.0, 2.3025851))
    rise = 1.3862944
    mixing = jax.random.uniform(key_mixing, (NB,), jnp.float32, 1.0, 2.0)
    shared = jnp.tile(common, (1, NB // 8)) * mixing[None, :]
    lower_rows = 0.25 * scales * (0.3 * shared + base)
    gains = jax.random.uniform(key_gain, (NB,), jnp.float32, 0.8, 1.25)
    leading = jax.random.uniform(key_top, (NB, NB), jnp.float32, -0.06, 0.06)
    identity = jnp.eye(NB, dtype=jnp.float32)
    leading = leading * (1.0 - identity) + identity * gains[None, :]
    values = jnp.concatenate([leading, lower_rows], axis=0)
    span = N // CYC_R
    holders = span // NB
    position = jnp.arange(N, dtype=jnp.int32)
    owner = (position % span // NB).astype(jnp.float32)
    ramp = jnp.exp(rise * owner / max(holders - 1, 1))
    values = values * ramp[:, None]
    return values.reshape(CYC_R, span, NB)


def draw_matrix(key, part):
    key = jax.random.fold_in(key, 23)
    key_base, key_scale = jax.random.split(key)
    base = jnp.clip(jax.random.normal(key_base, (N, N), jnp.float32), -6.0, 6.0)
    scales = jnp.exp(jax.random.uniform(key_scale, (N,), jnp.float32, -1.1512925, 1.1512925))
    scaled = base * scales[:, None] * scales[None, :]
    values = 0.70710678 * (scaled + scaled.T)
    return values.reshape(CYC_R, N // CYC_R, CYC_C, N // CYC_C)


def setup_inputs(seed: int = 0) -> dict:
    key_list = jax.random.split(jax.random.key(seed), 3)
    return {
        "panel": draw_panel(jax.random.fold_in(key_list[2], 71), 0),
        "matrix": draw_matrix(jax.random.fold_in(key_list[2], 71), 0),
    }


precise = lax.Precision.HIGHEST

def matmul(left, right):
    return jnp.dot(left.astype(jnp.float32), right.astype(jnp.float32), preferred_element_type=jnp.float32, precision=precise)

def right_solve(lower, values):
    return lax.linalg.triangular_solve(lower, values, left_side=False, lower=True, transpose_a=True)

def invert(square):
    normal = matmul(square.T, square)
    factor = jnp.linalg.cholesky(normal)
    middle = lax.linalg.triangular_solve(factor, square.T, left_side=True, lower=True)
    return lax.linalg.triangular_solve(factor, middle, left_side=True, lower=True, transpose_a=True)

def reference(panel, matrix):
    whole = panel.reshape(N, NB)
    square = matrix.reshape(N, N)
    lower_one = jnp.linalg.cholesky(matmul(whole.T, whole))
    basis = right_solve(lower_one, whole)
    r_factor = lower_one.T
    identity = jnp.eye(NB, dtype=jnp.float32)
    transform = invert(identity + basis[:NB].T)
    vectors = basis.at[:NB].add(identity)
    product = matmul(square, vectors)
    scaled = matmul(product, transform)
    coupling = matmul(transform.T, matmul(vectors.T, scaled))
    update = scaled - 0.5 * matmul(vectors, coupling)
    updated = square - matmul(update, vectors.T) - matmul(vectors, update.T)
    return (updated.reshape(matrix.shape), r_factor)
```

```python
import functools

import jax
import jax.numpy as jnp
from jax import lax
from jax.experimental import pallas as pl
from jax.experimental.pallas import tpu as pltpu
from jax.sharding import PartitionSpec as P

MESH = pl.DeviceIdType.MESH
precise = lax.Precision.HIGHEST
NX, NY, NZ = 4, 8, 8
NB = 256
PIECE = 16
SLICE = 32
VMEM_LIMIT = 40 * 1024 * 1024


def dot(left, right, contract=((1,), (0,))):
    return lax.dot_general(
        left, right, (contract, ((), ())), preferred_element_type=jnp.float32, precision=precise
    )


def remote(src, dst, send, recv, device):
    return pltpu.make_async_remote_copy(
        src_ref=src, dst_ref=dst, send_sem=send, recv_sem=recv, device_id=device, device_id_type=MESH
    )


class Place:
    def __init__(self):
        self.row = lax.axis_index("row")
        self.col = lax.axis_index("col")
        self.y, self.x = self.row // NX, self.row % NX
        self.z, self.core = self.col // 2, self.col % 2
        self.sibling = (self.row, 2 * self.z + 1 - self.core)
        self.half, self.turn = self.row // 16, self.row % 16
        self.partner = (16 * self.half + self.col, self.turn)
        self.alone = self.turn == self.col

    def at_x(self, step):
        return (NX * self.y + (self.x + step) % NX, self.col)

    def at_y(self, step):
        return (NX * ((self.y + step) % NY) + self.x, self.col)

    def at_z(self, step):
        return (self.row, 2 * ((self.z + step) % NZ) + self.core)

    def greet(self):
        barrier = pltpu.get_barrier_semaphore()
        devices = [self.at_x(s) for s in range(1, NX)]
        devices += [self.at_y(s) for s in range(1, NY)]
        devices += [self.at_z(s) for s in range(1, NZ)]
        devices += [self.sibling]
        for device in devices:
            pl.semaphore_signal(barrier, inc=1, device_id=device, device_id_type=MESH)

        @pl.when(jnp.logical_not(self.alone))
        def _():
            pl.semaphore_signal(barrier, inc=1, device_id=self.partner, device_id_type=MESH)
            pl.semaphore_wait(barrier, len(devices) + 1)

        @pl.when(self.alone)
        def _():
            pl.semaphore_wait(barrier, len(devices))


class Ring:
    def __init__(self, count, me, device, slot, send, recv):
        self.count, self.me, self.device, self.slot = count, me, device, slot
        self.send, self.recv = send, recv

    def copy(self, step, arriving):
        owner = (self.me - step) % self.count if arriving else self.me
        ref = self.slot(owner)
        return remote(ref, ref, self.send.at[step], self.recv.at[step], self.device(step))

    def start(self):
        for step in sorted(range(1, self.count), key=lambda s: -min(s, self.count - s)):
            self.copy(step, False).start()

    def order(self):
        return sorted(range(1, self.count), key=lambda s: min(s, self.count - s))

    def wait_recv(self):
        for step in self.order():
            self.copy(step, True).wait_recv()

    def wait_send(self):
        for step in range(1, self.count):
            self.copy(step, False).wait_send()


class Line(Ring):
    def __init__(self, here, slot, send, recv, pass_send, pass_recv):
        super().__init__(NZ, here.z, here.at_z, lambda z: slot(2 * z + here.core), send, recv)
        self.here, self.across = here, lambda z: slot(2 * z + 1 - here.core)
        self.pass_send, self.pass_recv = pass_send, pass_recv

    def hand(self, step, arriving):
        owner = (self.me - step) % self.count
        ref = self.across(owner) if arriving else self.slot(owner)
        return remote(ref, ref, self.pass_send.at[step], self.pass_recv.at[step], self.here.sibling)

    def start(self):
        super().start()
        self.hand(0, False).start()

    def finish(self):
        for step in self.order():
            self.copy(step, True).wait_recv()
            self.hand(step, False).start()
        for step in [0] + self.order():
            self.hand(step, True).wait_recv()

    def wait_send(self):
        super().wait_send()
        for step in range(self.count):
            self.hand(step, False).wait_send()


def place_of(y):
    return 4 * ((y % 4) // 2) + 2 * (y // 4) + y % 2


class Spread:
    def __init__(self, here, buffer, swap, y_send, y_recv, x_send, x_recv):
        self.here, self.buffer, self.swap = here, buffer, swap
        self.ring = Ring(
            NY, here.y, here.at_y, lambda y: buffer.at[place_of(y), here.x], y_send, y_recv
        )
        self.x_send, self.x_recv = x_send, x_recv

    def swap_copy(self, source, arriving):
        here = self.here
        row = here.row if arriving else here.partner[0]
        target = self.buffer.at[place_of(row // NX), row % NX]
        return remote(source, target, self.swap.at[0], self.swap.at[1], here.partner)

    def start(self, source):
        here = self.here

        @pl.when(jnp.logical_not(here.alone))
        def _():
            self.swap_copy(source, False).start()

        @pl.when(here.alone)
        def _():
            self.buffer[place_of(here.y), here.x] = source[...]

    def along_y(self, source):
        @pl.when(jnp.logical_not(self.here.alone))
        def _():
            self.swap_copy(source, True).wait_recv()

        self.ring.start()

    def x_copy(self, index, arriving):
        here = self.here
        part = (0, 1, 1, 0, 0, 1)[index]
        step = (1, 1, -1, -1, 1, -1)[index]
        owner = here.x if index < 4 else (here.x - step) % NX
        if arriving:
            owner = (owner - step) % NX
        ref = self.buffer.at[pl.ds(4 * part, 4), owner]
        return remote(ref, ref, self.x_send.at[index], self.x_recv.at[index], here.at_x(step))

    def along_x(self):
        self.ring.wait_recv()
        for index in (0, 2, 1, 3):
            self.x_copy(index, False).start()

    def finish(self):
        for first, then in ((0, 4), (2, 5)):
            self.x_copy(first, True).wait_recv()
            self.x_copy(then, False).start()
        for index in (1, 3, 4, 5):
            self.x_copy(index, True).wait_recv()

    def wait_send(self, source):
        @pl.when(jnp.logical_not(self.here.alone))
        def _():
            self.swap_copy(source, False).wait_send()

        self.ring.wait_send()
        for index in range(6):
            self.x_copy(index, False).wait_send()


class Total:
    def __init__(self, here, over_x, over_y, whole, sems):
        self.here, self.over_x, self.over_y, self.whole = here, over_x, over_y, whole
        x_send, x_recv, y_send, y_recv, z_send, z_recv, p_send, p_recv = sems
        self.xs = Ring(NX, here.x, here.at_x, lambda x: over_x.at[x], x_send, x_recv)
        self.ys = Ring(NY, here.y, here.at_y, lambda y: over_y.at[y], y_send, y_recv)
        self.zs = Line(here, lambda c: whole.at[c], z_send, z_recv, p_send, p_recv)

    def along_x(self, value):
        self.over_x[self.here.x] = value
        self.xs.start()

    def along_y(self):
        self.xs.wait_recv()
        value = (self.over_x[0] + self.over_x[1]) + (self.over_x[2] + self.over_x[3])
        self.over_y[self.here.y] = value
        self.ys.start()

    def along_z(self):
        self.ys.wait_recv()
        parts = [self.over_y[y] for y in range(NY)]
        while len(parts) > 1:
            parts = [a + b for a, b in zip(parts[::2], parts[1::2])]
        self.whole[self.here.col] = parts[0]
        self.zs.start()

    def finish(self):
        self.zs.finish()

    def wait_send(self):
        self.xs.wait_send()
        self.ys.wait_send()
        self.zs.wait_send()


TOTAL_SEMS = [pltpu.SemaphoreType.DMA((n,)) for n in (NX, NX, NY, NY, NZ, NZ, NZ, NZ)]
LINE_SEMS = [pltpu.SemaphoreType.DMA((NZ,)) for _ in range(4)]
SPREAD_SEMS = [pltpu.SemaphoreType.DMA((n,)) for n in (2, NY, NY, 6, 6)]


def first_kernel(
    piece, square, slab, columns, gram, top, share, corner,
    whole, over_x, over_y, result, other, arrivals, own, pair, core_sems, back_send, back_recv, corner_send, corner_recv,
    top_send, top_recv, *sems
):
    here = Place()
    line = Line(here, lambda c: whole.at[c], *sems[:4])
    spread = Spread(here, columns, *sems[4:9])
    total = Total(here, over_x, over_y, gram, sems[9:17])
    tops = Line(here, lambda c: top.at[c], *sems[17:21])
    here.greet()

    whole[here.col] = piece[...]
    line.start()

    def corner_copy(z, index):
        return remote(
            square.at[pl.ds(2 * SLICE * z, 2 * SLICE), pl.ds(0, NB)], pair,
            corner_send.at[index], corner_recv.at[0], (here.row, 2 * z),
        )

    def corner_hand():
        return remote(
            pair.at[pl.ds(SLICE, SLICE), :], corner, corner_send.at[NZ], corner_recv.at[1], here.sibling
        )

    @pl.when(here.col == 0)
    def _():
        for z in range(1, NZ):
            corner_copy(z, z).start()
        pair[...] = square[pl.ds(0, 2 * SLICE), pl.ds(0, NB)]

    line.finish()
    flipped = whole[...].reshape(NB, 2 * NB)
    slab[...] = flipped.T
    own[...] = slab[pl.ds(pl.multiple_of(SLICE * here.col, SLICE), SLICE), :]
    spread.start(own)
    total.along_x(dot(piece[...], slab[...]))

    def top_x(step):
        ref = top.at[here.col]
        return remote(ref, ref, top_send.at[step], top_recv.at[0], here.at_x(step))

    def top_y(step):
        ref = top.at[here.col]
        return remote(ref, ref, top_send.at[NX + step], top_recv.at[1], here.at_y(step))

    @pl.when(here.row == 0)
    def _():
        top[here.col] = slab[pl.ds(pl.multiple_of(PIECE * here.col, PIECE), PIECE), :]
        for step in range(1, NX):
            top_x(step).start()

    spread.along_y(own)

    @pl.when(here.y == 0)
    def _():
        @pl.when(here.x > 0)
        def _():
            top_x(1).wait_recv()

        for step in range(1, NY):
            top_y(step).start()

    total.along_y()
    spread.along_x()

    @pl.when(here.y > 0)
    def _():
        top_y(1).wait_recv()

    tops.start()
    total.along_z()
    spread.finish()

    partial = dot(square[...], columns[...].reshape(4 * NB, NB))
    result[...] = partial.reshape(NZ, 2, SLICE, NB)
    across = remote(
        result.at[:, 1 - here.core], other, core_sems.at[0], core_sems.at[1], here.sibling
    )
    across.start()

    @pl.when(here.core == 0)
    def _():
        @pl.when(here.z > 0)
        def _():
            corner_copy(here.z, 0).wait_recv()

        corner_hand().start()
        corner[...] = pair[pl.ds(0, SLICE), :]

    tops.finish()
    total.finish()
    across.wait_recv()
    across.wait_send()

    mine = arrivals.at[0]

    def back(step):
        return remote(
            other.at[(here.z + step) % NZ], arrivals.at[step],
            back_send.at[step], back_recv.at[step], here.at_z(step),
        )

    for z in range(NZ):
        other[z] = other[z] + result[z, here.core]
    for step in (4, 3, 5, 2, 6, 1, 7):
        back(step).start()
    value = other[here.z]
    for step in (1, 7, 2, 6, 3, 5, 4):
        back(step).wait_recv()
        value = value + arrivals[step]
    share[...] = value

    for step in range(1, NZ):
        back(step).wait_send()

    @pl.when(here.col == 0)
    def _():
        for z in range(1, NZ):
            corner_copy(z, z).wait_send()

    @pl.when(here.core == 0)
    def _():
        corner_hand().wait_send()

    @pl.when(here.core == 1)
    def _():
        corner_hand().wait_recv()

    @pl.when(here.row == 0)
    def _():
        for step in range(1, NX):
            top_x(step).wait_send()

    @pl.when(here.y == 0)
    def _():
        for step in range(1, NY):
            top_y(step).wait_send()

    line.wait_send()
    spread.wait_send(own)
    total.wait_send()
    tops.wait_send()


def second_kernel(
    slab, share, corner, inverse, transform, update, vectors, columns,
    product, over_x, over_y, coupling, own, *sems
):
    here = Place()
    line = Line(here, lambda c: product.at[c], *sems[:4])
    spread = Spread(here, columns, *sems[4:9])
    total = Total(here, over_x, over_y, coupling, sems[9:17])
    here.greet()

    product[here.col] = dot(share[...], inverse[...], ((1,), (1,))) + corner[...]
    line.start()
    basis = dot(slab[...], inverse[...], ((1,), (1,)))
    at_top = here.row == 0
    rows = lax.broadcasted_iota(jnp.int32, basis.shape, 0)
    cols = lax.broadcasted_iota(jnp.int32, basis.shape, 1)
    vectors[...] = basis + jnp.where(jnp.logical_and(rows == cols, at_top), 1.0, 0.0)
    begin = pl.multiple_of(PIECE * here.col, PIECE)
    flipped = dot(inverse[pl.ds(begin, PIECE), :], slab[...], ((1,), (1,)))
    rows = lax.broadcasted_iota(jnp.int32, flipped.shape, 0) + begin
    cols = lax.broadcasted_iota(jnp.int32, flipped.shape, 1)
    flipped = flipped + jnp.where(jnp.logical_and(rows == cols, at_top), 1.0, 0.0)
    line.finish()
    whole = product[...].reshape(2 * NB, NB)
    total.along_x(dot(flipped, whole))
    scaled = dot(whole, transform[...])
    total.along_y()
    total.along_z()
    total.finish()
    inner = dot(coupling[...].reshape(NB, NB), transform[...])
    middle = dot(transform[...], inner, ((0,), (0,)))
    update[...] = scaled - 0.5 * dot(vectors[...], middle)
    own[...] = update[pl.ds(pl.multiple_of(SLICE * here.col, SLICE), SLICE), :]
    spread.start(own)
    spread.along_y(own)
    spread.along_x()
    spread.finish()

    line.wait_send()
    spread.wait_send(own)
    total.wait_send()


def vmem(*shape):
    return jax.ShapeDtypeStruct(shape, jnp.float32)


def kernel_call(body, name, ident, outs, scratch, *args):
    whole = pl.BlockSpec(memory_space=pltpu.VMEM)
    return pl.pallas_call(
        body,
        out_shape=[vmem(*s) for s in outs],
        in_specs=[whole] * len(args),
        out_specs=[whole] * len(outs),
        scratch_shapes=scratch,
        compiler_params=pltpu.CompilerParams(
            collective_id=ident, has_side_effects=True, vmem_limit_bytes=VMEM_LIMIT
        ),
        name=name,
    )(*args)


def scratch(*shape):
    return pltpu.VMEM(shape, jnp.float32)


def dma(n):
    return pltpu.SemaphoreType.DMA((n,))


def matmul(left, right):
    return jnp.dot(left, right, preferred_element_type=jnp.float32, precision=precise)


def invert(square):
    normal = matmul(square.T, square)
    factor = jnp.linalg.cholesky(normal)
    middle = lax.linalg.triangular_solve(factor, square.T, left_side=True, lower=True)
    return lax.linalg.triangular_solve(factor, middle, left_side=True, lower=True, transpose_a=True)


def per_device(panel, matrix):
    square = matrix.reshape(2 * NB, 4 * NB)
    piece = panel.reshape(2 * NB, PIECE).T
    slab, columns, gram, top, share, corner = kernel_call(
        first_kernel, "first", 0,
        [(2 * NB, NB), (8, 4, SLICE, NB), (PIECE, PIECE, NB), (PIECE, PIECE, NB), (SLICE, NB), (SLICE, NB)],
        [
            scratch(PIECE, PIECE, 2 * NB), scratch(NX, PIECE, NB), scratch(NY, PIECE, NB),
            scratch(NZ, 2, SLICE, NB), scratch(NZ, SLICE, NB), scratch(NZ, SLICE, NB), scratch(SLICE, NB), scratch(2 * SLICE, NB),
            dma(2), dma(NZ), dma(NZ), dma(NZ + 1), dma(2), dma(NX + NY), dma(2),
            *LINE_SEMS, *SPREAD_SEMS, *TOTAL_SEMS, *LINE_SEMS,
        ],
        piece, square,
    )
    columns = columns.reshape(4 * NB, NB)
    identity = jnp.eye(NB, dtype=jnp.float32)
    lower_one = jnp.linalg.cholesky(gram.reshape(NB, NB))
    inverse = lax.linalg.triangular_solve(lower_one, identity, left_side=True, lower=True)
    leading = matmul(top.reshape(NB, NB), inverse.T)
    transform = invert(identity + leading.T)
    update, vectors, update_cols = kernel_call(
        second_kernel, "second", 1,
        [(2 * NB, NB), (2 * NB, NB), (8, 4, SLICE, NB)],
        [
            scratch(PIECE, SLICE, NB), scratch(NX, PIECE, NB), scratch(NY, PIECE, NB),
            scratch(PIECE, PIECE, NB), scratch(SLICE, NB),
            *LINE_SEMS, *SPREAD_SEMS, *TOTAL_SEMS,
        ],
        slab, share, corner, inverse, transform,
    )
    update_cols = update_cols.reshape(4 * NB, NB)
    first = (lax.axis_index("col") == 0).astype(jnp.float32)
    vectors_cols = dot(columns, inverse, ((1,), (1,))).at[:NB].add(identity * first)
    left = jnp.concatenate([update, vectors], axis=1)
    right = jnp.concatenate([vectors_cols, update_cols], axis=1)
    updated = square - dot(left, right, ((1,), (1,)))
    return (updated.reshape(matrix.shape), lower_one.T)


def solution(mesh):
    in_specs = (P(None, "row", "col"), P(None, "row", None, "col"))
    out_specs = (P(None, "row", None, "col"), P())
    return jax.shard_map(
        per_device, mesh=mesh, in_specs=in_specs, out_specs=out_specs, check_vma=False
    )
```

```python
import functools

import jax
import jax.numpy as jnp
from jax import lax
from jax.experimental import pallas as pl
from jax.experimental.pallas import tpu as pltpu
from jax.sharding import PartitionSpec as P

MESH = pl.DeviceIdType.MESH
precise = lax.Precision.HIGHEST
NX, NY, NZ = 4, 8, 8
NB = 256
PIECE = 16
SLICE = 32
VMEM_LIMIT = 40 * 1024 * 1024


def dot(left, right, contract=((1,), (0,))):
    return lax.dot_general(
        left, right, (contract, ((), ())), preferred_element_type=jnp.float32, precision=precise
    )


def remote(src, dst, send, recv, device):
    return pltpu.make_async_remote_copy(
        src_ref=src, dst_ref=dst, send_sem=send, recv_sem=recv, device_id=device, device_id_type=MESH
    )


class Place:
    def __init__(self):
        self.row = lax.axis_index("row")
        self.col = lax.axis_index("col")
        self.y, self.x = self.row // NX, self.row % NX
        self.z, self.core = self.col // 2, self.col % 2
        self.sibling = (self.row, 2 * self.z + 1 - self.core)
        self.half, self.turn = self.row // 16, self.row % 16
        self.partner = (16 * self.half + self.col, self.turn)
        self.alone = self.turn == self.col

    def at_x(self, step):
        return (NX * self.y + (self.x + step) % NX, self.col)

    def at_y(self, step):
        return (NX * ((self.y + step) % NY) + self.x, self.col)

    def at_z(self, step):
        return (self.row, 2 * ((self.z + step) % NZ) + self.core)

    def greet(self):
        barrier = pltpu.get_barrier_semaphore()
        devices = [self.at_x(s) for s in range(1, NX)]
        devices += [self.at_y(s) for s in range(1, NY)]
        devices += [self.at_z(s) for s in range(1, NZ)]
        devices += [self.sibling]
        for device in devices:
            pl.semaphore_signal(barrier, inc=1, device_id=device, device_id_type=MESH)

        @pl.when(jnp.logical_not(self.alone))
        def _():
            pl.semaphore_signal(barrier, inc=1, device_id=self.partner, device_id_type=MESH)
            pl.semaphore_wait(barrier, len(devices) + 1)

        @pl.when(self.alone)
        def _():
            pl.semaphore_wait(barrier, len(devices))


class Ring:
    def __init__(self, count, me, device, slot, send, recv):
        self.count, self.me, self.device, self.slot = count, me, device, slot
        self.send, self.recv = send, recv

    def copy(self, step, arriving):
        owner = (self.me - step) % self.count if arriving else self.me
        ref = self.slot(owner)
        return remote(ref, ref, self.send.at[step], self.recv.at[step], self.device(step))

    def start(self):
        for step in sorted(range(1, self.count), key=lambda s: -min(s, self.count - s)):
            self.copy(step, False).start()

    def order(self):
        return sorted(range(1, self.count), key=lambda s: min(s, self.count - s))

    def wait_recv(self):
        for step in self.order():
            self.copy(step, True).wait_recv()

    def wait_send(self):
        for step in range(1, self.count):
            self.copy(step, False).wait_send()


class Line(Ring):
    def __init__(self, here, slot, send, recv, pass_send, pass_recv):
        super().__init__(NZ, here.z, here.at_z, lambda z: slot(2 * z + here.core), send, recv)
        self.here, self.across = here, lambda z: slot(2 * z + 1 - here.core)
        self.pass_send, self.pass_recv = pass_send, pass_recv

    def hand(self, step, arriving):
        owner = (self.me - step) % self.count
        ref = self.across(owner) if arriving else self.slot(owner)
        return remote(ref, ref, self.pass_send.at[step], self.pass_recv.at[step], self.here.sibling)

    def start(self):
        super().start()
        self.hand(0, False).start()

    def finish(self):
        for step in self.order():
            self.copy(step, True).wait_recv()
            self.hand(step, False).start()
        for step in [0] + self.order():
            self.hand(step, True).wait_recv()

    def wait_send(self):
        super().wait_send()
        for step in range(self.count):
            self.hand(step, False).wait_send()


def place_of(y):
    return 4 * ((y % 4) // 2) + 2 * (y // 4) + y % 2


class Spread:
    def __init__(self, here, buffer, swap, y_send, y_recv, x_send, x_recv):
        self.here, self.buffer, self.swap = here, buffer, swap
        self.ring = Ring(
            NY, here.y, here.at_y, lambda y: buffer.at[place_of(y), here.x], y_send, y_recv
        )
        self.x_send, self.x_recv = x_send, x_recv

    def swap_copy(self, source, arriving):
        here = self.here
        row = here.row if arriving else here.partner[0]
        target = self.buffer.at[place_of(row // NX), row % NX]
        return remote(source, target, self.swap.at[0], self.swap.at[1], here.partner)

    def start(self, source):
        here = self.here

        @pl.when(jnp.logical_not(here.alone))
        def _():
            self.swap_copy(source, False).start()

        @pl.when(here.alone)
        def _():
            self.buffer[place_of(here.y), here.x] = source[...]

    def along_y(self, source):
        @pl.when(jnp.logical_not(self.here.alone))
        def _():
            self.swap_copy(source, True).wait_recv()

        self.ring.start()

    def x_copy(self, index, arriving):
        here = self.here
        part = (0, 1, 1, 0, 0, 1)[index]
        step = (1, 1, -1, -1, 1, -1)[index]
        owner = here.x if index < 4 else (here.x - step) % NX
        if arriving:
            owner = (owner - step) % NX
        ref = self.buffer.at[pl.ds(4 * part, 4), owner]
        return remote(ref, ref, self.x_send.at[index], self.x_recv.at[index], here.at_x(step))

    def along_x(self):
        self.ring.wait_recv()
        for index in (0, 2, 1, 3):
            self.x_copy(index, False).start()

    def finish(self):
        for first, then in ((0, 4), (2, 5)):
            self.x_copy(first, True).wait_recv()
            self.x_copy(then, False).start()
        for index in (1, 3, 4, 5):
            self.x_copy(index, True).wait_recv()

    def wait_send(self, source):
        @pl.when(jnp.logical_not(self.here.alone))
        def _():
            self.swap_copy(source, False).wait_send()

        self.ring.wait_send()
        for index in range(6):
            self.x_copy(index, False).wait_send()


class Total:
    def __init__(self, here, over_x, over_y, whole, sems):
        self.here, self.over_x, self.over_y, self.whole = here, over_x, over_y, whole
        x_send, x_recv, y_send, y_recv, z_send, z_recv, p_send, p_recv = sems
        self.xs = Ring(NX, here.x, here.at_x, lambda x: over_x.at[x], x_send, x_recv)
        self.ys = Ring(NY, here.y, here.at_y, lambda y: over_y.at[y], y_send, y_recv)
        self.zs = Line(here, lambda c: whole.at[c], z_send, z_recv, p_send, p_recv)

    def along_x(self, value):
        self.over_x[self.here.x] = value
        self.xs.start()

    def along_y(self):
        self.xs.wait_recv()
        value = (self.over_x[0] + self.over_x[1]) + (self.over_x[2] + self.over_x[3])
        self.over_y[self.here.y] = value
        self.ys.start()

    def along_z(self):
        self.ys.wait_recv()
        parts = [self.over_y[y] for y in range(NY)]
        while len(parts) > 1:
            parts = [a + b for a, b in zip(parts[::2], parts[1::2])]
        self.whole[self.here.col] = parts[0]
        self.zs.start()

    def finish(self):
        self.zs.finish()

    def wait_send(self):
        self.xs.wait_send()
        self.ys.wait_send()
        self.zs.wait_send()


TOTAL_SEMS = [pltpu.SemaphoreType.DMA((n,)) for n in (NX, NX, NY, NY, NZ, NZ, NZ, NZ)]
LINE_SEMS = [pltpu.SemaphoreType.DMA((NZ,)) for _ in range(4)]
SPREAD_SEMS = [pltpu.SemaphoreType.DMA((n,)) for n in (2, NY, NY, 6, 6)]


def first_kernel(
    piece, square, slab, columns, gram, top, share, corner,
    whole, over_x, over_y, result, other, arrivals, own, pair, core_sems, back_send, back_recv, corner_send, corner_recv,
    top_send, top_recv, *sems
):
    here = Place()
    line = Line(here, lambda c: whole.at[c], *sems[:4])
    spread = Spread(here, columns, *sems[4:9])
    total = Total(here, over_x, over_y, gram, sems[9:17])
    tops = Line(here, lambda c: top.at[c], *sems[17:21])
    here.greet()

    whole[here.col] = piece[...]
    line.start()

    def corner_copy(z, index):
        return remote(
            square.at[pl.ds(2 * SLICE * z, 2 * SLICE), pl.ds(0, NB)], pair,
            corner_send.at[index], corner_recv.at[0], (here.row, 2 * z),
        )

    def corner_hand():
        return remote(
            pair.at[pl.ds(SLICE, SLICE), :], corner, corner_send.at[NZ], corner_recv.at[1], here.sibling
        )

    @pl.when(here.col == 0)
    def _():
        for z in range(1, NZ):
            corner_copy(z, z).start()
        pair[...] = square[pl.ds(0, 2 * SLICE), pl.ds(0, NB)]

    line.finish()
    flipped = whole[...].reshape(NB, 2 * NB)
    slab[...] = flipped.T
    own[...] = slab[pl.ds(pl.multiple_of(SLICE * here.col, SLICE), SLICE), :]
    spread.start(own)
    total.along_x(dot(piece[...], slab[...]))

    def top_x(step):
        ref = top.at[here.col]
        return remote(ref, ref, top_send.at[step], top_recv.at[0], here.at_x(step))

    def top_y(step):
        ref = top.at[here.col]
        return remote(ref, ref, top_send.at[NX + step], top_recv.at[1], here.at_y(step))

    @pl.when(here.row == 0)
    def _():
        top[here.col] = slab[pl.ds(pl.multiple_of(PIECE * here.col, PIECE), PIECE), :]
        for step in range(1, NX):
            top_x(step).start()

    spread.along_y(own)

    @pl.when(here.y == 0)
    def _():
        @pl.when(here.x > 0)
        def _():
            top_x(1).wait_recv()

        for step in range(1, NY):
            top_y(step).start()

    total.along_y()
    spread.along_x()

    @pl.when(here.y > 0)
    def _():
        top_y(1).wait_recv()

    tops.start()
    total.along_z()
    spread.finish()

    partial = dot(square[...], columns[...].reshape(4 * NB, NB))
    result[...] = partial.reshape(NZ, 2, SLICE, NB)
    across = remote(
        result.at[:, 1 - here.core], other, core_sems.at[0], core_sems.at[1], here.sibling
    )
    across.start()

    @pl.when(here.core == 0)
    def _():
        @pl.when(here.z > 0)
        def _():
            corner_copy(here.z, 0).wait_recv()

        corner_hand().start()
        corner[...] = pair[pl.ds(0, SLICE), :]

    tops.finish()
    total.finish()
    across.wait_recv()
    across.wait_send()

    mine = arrivals.at[0]

    def back(step):
        return remote(
            other.at[(here.z + step) % NZ], arrivals.at[step],
            back_send.at[step], back_recv.at[step], here.at_z(step),
        )

    for z in range(NZ):
        other[z] = other[z] + result[z, here.core]
    for step in (4, 3, 5, 2, 6, 1, 7):
        back(step).start()
    value = other[here.z]
    for step in (1, 7, 2, 6, 3, 5, 4):
        back(step).wait_recv()
        value = value + arrivals[step]
    share[...] = value

    for step in range(1, NZ):
        back(step).wait_send()

    @pl.when(here.col == 0)
    def _():
        for z in range(1, NZ):
            corner_copy(z, z).wait_send()

    @pl.when(here.core == 0)
    def _():
        corner_hand().wait_send()

    @pl.when(here.core == 1)
    def _():
        corner_hand().wait_recv()

    @pl.when(here.row == 0)
    def _():
        for step in range(1, NX):
            top_x(step).wait_send()

    @pl.when(here.y == 0)
    def _():
        for step in range(1, NY):
            top_y(step).wait_send()

    line.wait_send()
    spread.wait_send(own)
    total.wait_send()
    tops.wait_send()


def second_kernel(
    slab, share, corner, inverse, transform, update, vectors, columns,
    product, over_x, over_y, coupling, own, *sems
):
    here = Place()
    line = Line(here, lambda c: product.at[c], *sems[:4])
    spread = Spread(here, columns, *sems[4:9])
    total = Total(here, over_x, over_y, coupling, sems[9:17])
    here.greet()

    product[here.col] = dot(share[...], inverse[...], ((1,), (1,))) + corner[...]
    line.start()
    basis = dot(slab[...], inverse[...], ((1,), (1,)))
    at_top = here.row == 0
    rows = lax.broadcasted_iota(jnp.int32, basis.shape, 0)
    cols = lax.broadcasted_iota(jnp.int32, basis.shape, 1)
    vectors[...] = basis + jnp.where(jnp.logical_and(rows == cols, at_top), 1.0, 0.0)
    begin = pl.multiple_of(PIECE * here.col, PIECE)
    flipped = dot(inverse[pl.ds(begin, PIECE), :], slab[...], ((1,), (1,)))
    rows = lax.broadcasted_iota(jnp.int32, flipped.shape, 0) + begin
    cols = lax.broadcasted_iota(jnp.int32, flipped.shape, 1)
    flipped = flipped + jnp.where(jnp.logical_and(rows == cols, at_top), 1.0, 0.0)
    line.finish()
    whole = product[...].reshape(2 * NB, NB)
    total.along_x(dot(flipped, whole))
    scaled = dot(whole, transform[...])
    total.along_y()
    total.along_z()
    total.finish()
    inner = dot(coupling[...].reshape(NB, NB), transform[...])
    middle = dot(transform[...], inner, ((0,), (0,)))
    update[...] = scaled - 0.5 * dot(vectors[...], middle)
    own[...] = update[pl.ds(pl.multiple_of(SLICE * here.col, SLICE), SLICE), :]
    spread.start(own)
    spread.along_y(own)
    spread.along_x()
    spread.finish()

    line.wait_send()
    spread.wait_send(own)
    total.wait_send()


LANES, GROUP, STEP = 128, 32, 8


def columns_of(block, begin, rows):
    return [jnp.broadcast_to(block[:, begin + l : begin + l + 1], (rows, LANES)) for l in range(STEP)]


def factor_kernel(gram, top, upper, inverse, transform, work, pad):
    lane = lax.broadcasted_iota(jnp.int32, (GROUP, LANES), 1)
    line = lax.broadcasted_iota(jnp.int32, (GROUP, LANES), 0)
    rows_all = lax.broadcasted_iota(jnp.int32, (NB, NB), 0)
    cols_all = lax.broadcasted_iota(jnp.int32, (NB, NB), 1)
    identity = jnp.where(rows_all == cols_all, 1.0, 0.0)
    work[:, :NB] = gram[...]
    work[:, NB:] = identity
    for base in range(0, NB, GROUP):
        first, last = base // LANES, 2 + base // LANES + 1
        blocks = {q: work[base : base + GROUP, LANES * q : LANES * (q + 1)] for q in range(first, last)}
        for sub in range(0, GROUP, STEP):
            count = GROUP - sub
            number = line[:count]
            cols = columns_of(blocks[first], (base + sub) % LANES, count)
            scale = jnp.ones((STEP, LANES), jnp.float32)
            for j in range(STEP):
                pivot = cols[j][j : j + 1]
                over = 1.0 / pivot
                scale = jnp.where(number[:STEP] == j, lax.rsqrt(pivot), scale)
                factor = jnp.where(number > j, cols[j] * over, 0.0)
                for l in range(j + 1, STEP):
                    cols[l] = cols[l] - factor * cols[l][j : j + 1]
                for q in blocks:
                    blocks[q] = blocks[q] - factor * blocks[q][j : j + 1]
            for q in blocks:
                work[base + sub : base + sub + STEP, LANES * q : LANES * (q + 1)] = blocks[q][:STEP] * scale
                blocks[q] = blocks[q][STEP:]
        after = base + GROUP
        if after < NB:
            start = after // LANES
            left = work[base:after, LANES * start : NB]
            right = work[base:after, LANES * start : LANES * last]
            change = dot(left, right, ((0,), (0,)))
            work[after:, LANES * start : LANES * last] -= change[after - LANES * start :]
    upper[...] = jnp.where(rows_all <= cols_all, work[:, :NB], 0.0)
    inverse[...] = work[:, NB:]
    transform[...] = dot(inverse[...], top[...], ((1,), (1,))) + identity
    pad[...] = jnp.zeros_like(pad)
    lane_all = lax.broadcasted_iota(jnp.int32, (NB, LANES), 1)
    for base in range(0, NB, GROUP):
        home, offset = base // LANES, base % LANES
        blocks = {q: transform[base : base + GROUP, LANES * q : LANES * (q + 1)] for q in range(2)}
        blocks[2] = jnp.where(lane == line + offset, 1.0, 0.0)
        scale = jnp.ones((GROUP, LANES), jnp.float32)
        for sub in range(0, GROUP, STEP):
            cols = columns_of(blocks[home], offset + sub, GROUP)
            for j in range(STEP):
                row = sub + j
                over = 1.0 / cols[j][row : row + 1]
                scale = jnp.where(line == row, over, scale)
                factor = jnp.where(line == row, 0.0, cols[j] * over)
                for l in range(j + 1, STEP):
                    cols[l] = cols[l] - factor * cols[l][row : row + 1]
                for q in blocks:
                    blocks[q] = blocks[q] - factor * blocks[q][row : row + 1]
        inside = jnp.logical_and(lane >= offset, lane < offset + GROUP)
        blocks = {q: blocks[q] * scale for q in blocks}
        blocks[home] = jnp.where(inside, blocks[2], blocks[home])
        for q in range(2):
            pad[offset : offset + GROUP, LANES * q : LANES * (q + 1)] = blocks[q]
        mine = transform[:, LANES * home : LANES * (home + 1)]
        inside_all = jnp.logical_and(lane_all >= offset, lane_all < offset + GROUP)
        change = dot(jnp.where(inside_all, mine, 0.0), pad[...])
        transform[:, LANES * home : LANES * (home + 1)] = jnp.where(inside_all, 0.0, mine)
        transform[...] -= change
        transform[base : base + GROUP, :] = pad[offset : offset + GROUP, :]
        pad[offset : offset + GROUP, :] = jnp.zeros((GROUP, NB), jnp.float32)

def vmem(*shape):
    return jax.ShapeDtypeStruct(shape, jnp.float32)


def kernel_call(body, name, ident, outs, scratch, *args):
    whole = pl.BlockSpec(memory_space=pltpu.VMEM)
    return pl.pallas_call(
        body,
        out_shape=[vmem(*s) for s in outs],
        in_specs=[whole] * len(args),
        out_specs=[whole] * len(outs),
        scratch_shapes=scratch,
        compiler_params=pltpu.CompilerParams(
            collective_id=ident, has_side_effects=True, vmem_limit_bytes=VMEM_LIMIT
        ),
        name=name,
    )(*args)


def scratch(*shape):
    return pltpu.VMEM(shape, jnp.float32)


def dma(n):
    return pltpu.SemaphoreType.DMA((n,))


def factor(gram, top):
    whole = pl.BlockSpec(memory_space=pltpu.VMEM)
    return pl.pallas_call(
        factor_kernel,
        out_shape=[vmem(NB, NB)] * 3,
        in_specs=[whole] * 2,
        out_specs=[whole] * 3,
        scratch_shapes=[scratch(NB, 2 * NB), scratch(LANES, NB)],
        compiler_params=pltpu.CompilerParams(vmem_limit_bytes=VMEM_LIMIT),
        name="factor",
    )(gram, top)


def per_device(panel, matrix):
    square = matrix.reshape(2 * NB, 4 * NB)
    piece = panel.reshape(2 * NB, PIECE).T
    slab, columns, gram, top, share, corner = kernel_call(
        first_kernel, "first", 0,
        [(2 * NB, NB), (8, 4, SLICE, NB), (PIECE, PIECE, NB), (PIECE, PIECE, NB), (SLICE, NB), (SLICE, NB)],
        [
            scratch(PIECE, PIECE, 2 * NB), scratch(NX, PIECE, NB), scratch(NY, PIECE, NB),
            scratch(NZ, 2, SLICE, NB), scratch(NZ, SLICE, NB), scratch(NZ, SLICE, NB), scratch(SLICE, NB), scratch(2 * SLICE, NB),
            dma(2), dma(NZ), dma(NZ), dma(NZ + 1), dma(2), dma(NX + NY), dma(2),
            *LINE_SEMS, *SPREAD_SEMS, *TOTAL_SEMS, *LINE_SEMS,
        ],
        piece, square,
    )
    columns = columns.reshape(4 * NB, NB)
    identity = jnp.eye(NB, dtype=jnp.float32)
    upper, inverse, transform = factor(gram.reshape(NB, NB), top.reshape(NB, NB))
    update, vectors, update_cols = kernel_call(
        second_kernel, "second", 1,
        [(2 * NB, NB), (2 * NB, NB), (8, 4, SLICE, NB)],
        [
            scratch(PIECE, SLICE, NB), scratch(NX, PIECE, NB), scratch(NY, PIECE, NB),
            scratch(PIECE, PIECE, NB), scratch(SLICE, NB),
            *LINE_SEMS, *SPREAD_SEMS, *TOTAL_SEMS,
        ],
        slab, share, corner, inverse, transform,
    )
    update_cols = update_cols.reshape(4 * NB, NB)
    first = (lax.axis_index("col") == 0).astype(jnp.float32)
    vectors_cols = dot(columns, inverse, ((1,), (1,))).at[:NB].add(identity * first)
    left = jnp.concatenate([update, vectors], axis=1)
    right = jnp.concatenate([vectors_cols, update_cols], axis=1)
    updated = square - dot(left, right, ((1,), (1,)))
    return (updated.reshape(matrix.shape), upper)


def solution(mesh):
    in_specs = (P(None, "row", "col"), P(None, "row", None, "col"))
    out_specs = (P(None, "row", None, "col"), P())
    return jax.shard_map(
        per_device, mesh=mesh, in_specs=in_specs, out_specs=out_specs, check_vma=False
    )
```

```python
import functools

import jax
import jax.numpy as jnp
from jax import lax
from jax.experimental import pallas as pl
from jax.experimental.pallas import tpu as pltpu
from jax.sharding import PartitionSpec as P

MESH = pl.DeviceIdType.MESH
precise = lax.Precision.HIGHEST
NX, NY, NZ = 4, 8, 8
NB = 256
PIECE = 16
SLICE = 32
VMEM_LIMIT = 40 * 1024 * 1024


def dot(left, right, contract=((1,), (0,))):
    return lax.dot_general(
        left, right, (contract, ((), ())), preferred_element_type=jnp.float32, precision=precise
    )


def remote(src, dst, send, recv, device):
    return pltpu.make_async_remote_copy(
        src_ref=src, dst_ref=dst, send_sem=send, recv_sem=recv, device_id=device, device_id_type=MESH
    )


class Place:
    def __init__(self):
        self.row = lax.axis_index("row")
        self.col = lax.axis_index("col")
        self.y, self.x = self.row // NX, self.row % NX
        self.z, self.core = self.col // 2, self.col % 2
        self.sibling = (self.row, 2 * self.z + 1 - self.core)
        self.half, self.turn = self.row // 16, self.row % 16
        self.partner = (16 * self.half + self.col, self.turn)
        self.alone = self.turn == self.col

    def at_x(self, step):
        return (NX * self.y + (self.x + step) % NX, self.col)

    def at_y(self, step):
        return (NX * ((self.y + step) % NY) + self.x, self.col)

    def at_z(self, step):
        return (self.row, 2 * ((self.z + step) % NZ) + self.core)

    def greet(self):
        barrier = pltpu.get_barrier_semaphore()
        devices = [self.at_x(s) for s in range(1, NX)]
        devices += [self.at_y(s) for s in range(1, NY)]
        devices += [self.at_z(s) for s in range(1, NZ)]
        devices += [self.sibling]
        for device in devices:
            pl.semaphore_signal(barrier, inc=1, device_id=device, device_id_type=MESH)

        @pl.when(jnp.logical_not(self.alone))
        def _():
            pl.semaphore_signal(barrier, inc=1, device_id=self.partner, device_id_type=MESH)
            pl.semaphore_wait(barrier, len(devices) + 1)

        @pl.when(self.alone)
        def _():
            pl.semaphore_wait(barrier, len(devices))


class Ring:
    def __init__(self, count, me, device, slot, send, recv):
        self.count, self.me, self.device, self.slot = count, me, device, slot
        self.send, self.recv = send, recv

    def copy(self, step, arriving):
        owner = (self.me - step) % self.count if arriving else self.me
        ref = self.slot(owner)
        return remote(ref, ref, self.send.at[step], self.recv.at[step], self.device(step))

    def start(self):
        for step in sorted(range(1, self.count), key=lambda s: -min(s, self.count - s)):
            self.copy(step, False).start()

    def order(self):
        return sorted(range(1, self.count), key=lambda s: min(s, self.count - s))

    def wait_recv(self):
        for step in self.order():
            self.copy(step, True).wait_recv()

    def wait_send(self):
        for step in range(1, self.count):
            self.copy(step, False).wait_send()


class Line(Ring):
    def __init__(self, here, slot, send, recv, pass_send, pass_recv):
        super().__init__(NZ, here.z, here.at_z, lambda z: slot(2 * z + here.core), send, recv)
        self.here, self.across = here, lambda z: slot(2 * z + 1 - here.core)
        self.pass_send, self.pass_recv = pass_send, pass_recv

    def hand(self, step, arriving):
        owner = (self.me - step) % self.count
        ref = self.across(owner) if arriving else self.slot(owner)
        return remote(ref, ref, self.pass_send.at[step], self.pass_recv.at[step], self.here.sibling)

    def start(self):
        super().start()
        self.hand(0, False).start()

    def finish(self):
        for step in self.order():
            self.copy(step, True).wait_recv()
            self.hand(step, False).start()
        for step in [0] + self.order():
            self.hand(step, True).wait_recv()

    def wait_send(self):
        super().wait_send()
        for step in range(self.count):
            self.hand(step, False).wait_send()


def place_of(y):
    return 4 * ((y % 4) // 2) + 2 * (y // 4) + y % 2


class Spread:
    def __init__(self, here, buffer, y_send, y_recv, x_send, x_recv):
        self.here, self.buffer = here, buffer
        self.ring = Ring(
            NY, here.y, here.at_y, lambda y: buffer.at[place_of(y), here.x], y_send, y_recv
        )
        self.x_send, self.x_recv = x_send, x_recv

    def along_y(self):
        self.ring.start()

    def x_copy(self, index, arriving):
        here = self.here
        part = (0, 1, 1, 0, 0, 1)[index]
        step = (1, 1, -1, -1, 1, -1)[index]
        owner = here.x if index < 4 else (here.x - step) % NX
        if arriving:
            owner = (owner - step) % NX
        ref = self.buffer.at[pl.ds(4 * part, 4), owner]
        return remote(ref, ref, self.x_send.at[index], self.x_recv.at[index], here.at_x(step))

    def along_x(self):
        self.ring.wait_recv()
        for index in (0, 2, 1, 3):
            self.x_copy(index, False).start()

    def forward(self):
        for first, then in ((0, 4), (2, 5)):
            self.x_copy(first, True).wait_recv()
            self.x_copy(then, False).start()

    def finish(self):
        for index in (1, 3, 4, 5):
            self.x_copy(index, True).wait_recv()

    def wait_send(self):
        self.ring.wait_send()
        for index in range(6):
            self.x_copy(index, False).wait_send()


class Swap:
    def __init__(self, here, source, target_at, sems):
        self.here, self.source, self.target_at, self.sems = here, source, target_at, sems

    def copy(self, arriving):
        here = self.here
        target = self.target_at(*((here.row, here.col) if arriving else here.partner))
        return remote(self.source, target, self.sems.at[0], self.sems.at[1], here.partner)

    def start(self):
        @pl.when(jnp.logical_not(self.here.alone))
        def _():
            self.copy(False).start()

        @pl.when(self.here.alone)
        def _():
            self.target_at(self.here.row, self.here.col)[...] = self.source[...]

    def wait_recv(self):
        @pl.when(jnp.logical_not(self.here.alone))
        def _():
            self.copy(True).wait_recv()

    def wait_send(self):
        @pl.when(jnp.logical_not(self.here.alone))
        def _():
            self.copy(False).wait_send()


class Total:
    def __init__(self, here, over_x, over_y, whole, sems):
        self.here, self.over_x, self.over_y, self.whole = here, over_x, over_y, whole
        x_send, x_recv, y_send, y_recv, z_send, z_recv, p_send, p_recv = sems
        self.xs = Ring(NX, here.x, here.at_x, lambda x: over_x.at[x], x_send, x_recv)
        self.ys = Ring(NY, here.y, here.at_y, lambda y: over_y.at[y], y_send, y_recv)
        self.zs = Line(here, lambda c: whole.at[c], z_send, z_recv, p_send, p_recv)

    def along_x(self, value):
        self.over_x[self.here.x] = value
        self.xs.start()

    def along_y(self):
        self.xs.wait_recv()
        value = (self.over_x[0] + self.over_x[1]) + (self.over_x[2] + self.over_x[3])
        self.over_y[self.here.y] = value
        self.ys.start()

    def along_z(self):
        self.ys.wait_recv()
        parts = [self.over_y[y] for y in range(NY)]
        while len(parts) > 1:
            parts = [a + b for a, b in zip(parts[::2], parts[1::2])]
        self.whole[self.here.col] = parts[0]
        self.zs.start()

    def finish(self):
        self.zs.finish()

    def wait_send(self):
        self.xs.wait_send()
        self.ys.wait_send()
        self.zs.wait_send()


class PlaneSum:
    def __init__(self, here, terms, early, late, kept, arrivals, x_send, x_recv, y_send, y_recv):
        self.here, self.terms, self.early, self.late = here, terms, early, late
        self.kept, self.arrivals = kept, arrivals
        self.x_send, self.x_recv, self.y_send, self.y_recv = x_send, x_recv, y_send, y_recv

    def x_copy(self, index):
        here, way = self.here, index % 2
        step = 1 - 2 * way
        half = (way, 1 - way, way)[index // 2]
        owner = (here.x + (2 if index < 2 else step)) % NX
        source = self.terms.at[pl.ds(4 * half, 4), owner]
        target = self.early.at[way] if index < 2 else self.late.at[way, pl.ds(4 * half, 4)]
        return remote(source, target, self.x_send.at[index], self.x_recv.at[index], here.at_x(step))

    def start(self):
        for index in range(4):
            self.x_copy(index).start()

    def combine(self):
        for way in range(2):
            self.x_copy(way).wait_recv()
            owner = (self.here.x + 1 - 2 * way) % NX
            self.terms[pl.ds(4 * way, 4), owner] = self.terms[pl.ds(4 * way, 4), owner] + self.early[way]
            self.x_copy(4 + way).start()

    def y_copy(self, step):
        return remote(
            self.kept.at[place_of((self.here.y + step) % NY)], self.arrivals.at[step],
            self.y_send.at[step], self.y_recv.at[step], self.here.at_y(step),
        )

    def along_y(self):
        for index in range(2, 6):
            self.x_copy(index).wait_recv()
        self.kept[...] = self.terms[:, self.here.x] + (self.late[0] + self.late[1])
        for step in (4, 3, 5, 2, 6, 1, 7):
            self.y_copy(step).start()

    def finish(self):
        value = self.kept[place_of(self.here.y)]
        for step in (1, 7, 2, 6, 3, 5, 4):
            self.y_copy(step).wait_recv()
            value = value + self.arrivals[step]
        return value

    def wait_send(self):
        for index in range(6):
            self.x_copy(index).wait_send()
        for step in range(1, NY):
            self.y_copy(step).wait_send()


LANES, GROUP, STEP = 128, 32, 8


def columns_of(block, begin, rows):
    return [jnp.broadcast_to(block[:, begin + l : begin + l + 1], (rows, LANES)) for l in range(STEP)]


def cholesky_panels(gram, upper, inverse, work):
    line = lax.broadcasted_iota(jnp.int32, (GROUP, LANES), 0)
    rows_all = lax.broadcasted_iota(jnp.int32, (NB, NB), 0)
    cols_all = lax.broadcasted_iota(jnp.int32, (NB, NB), 1)
    work[:, :NB] = gram
    work[:, NB:] = jnp.where(rows_all == cols_all, 1.0, 0.0)
    for base in range(0, NB, GROUP):
        first, last = base // LANES, 2 + base // LANES + 1
        blocks = {q: work[base : base + GROUP, LANES * q : LANES * (q + 1)] for q in range(first, last)}
        for sub in range(0, GROUP, STEP):
            count = GROUP - sub
            number = line[:count]
            cols = columns_of(blocks[first], (base + sub) % LANES, count)
            scale = jnp.ones((STEP, LANES), jnp.float32)
            for j in range(STEP):
                pivot = cols[j][j : j + 1]
                over = 1.0 / pivot
                scale = jnp.where(number[:STEP] == j, lax.rsqrt(pivot), scale)
                factor = jnp.where(number > j, cols[j] * over, 0.0)
                for l in range(j + 1, STEP):
                    cols[l] = cols[l] - factor * cols[l][j : j + 1]
                for q in blocks:
                    blocks[q] = blocks[q] - factor * blocks[q][j : j + 1]
            for q in blocks:
                work[base + sub : base + sub + STEP, LANES * q : LANES * (q + 1)] = blocks[q][:STEP] * scale
                blocks[q] = blocks[q][STEP:]
        after = base + GROUP
        if after < NB:
            start = after // LANES
            left = work[base:after, LANES * start : NB]
            right = work[base:after, LANES * start : LANES * last]
            change = dot(left, right, ((0,), (0,)))
            work[after:, LANES * start : LANES * last] -= change[after - LANES * start :]
        else:
            upper[...] = jnp.where(rows_all <= cols_all, work[:, :NB], 0.0)
            inverse[...] = work[:, NB:]
        yield base // GROUP


def inverse_panels(square, pad):
    lane = lax.broadcasted_iota(jnp.int32, (GROUP, LANES), 1)
    line = lax.broadcasted_iota(jnp.int32, (GROUP, LANES), 0)
    pad[...] = jnp.zeros_like(pad)
    lane_all = lax.broadcasted_iota(jnp.int32, (NB, LANES), 1)
    for base in range(0, NB, GROUP):
        home, offset = base // LANES, base % LANES
        blocks = {q: square[base : base + GROUP, LANES * q : LANES * (q + 1)] for q in range(2)}
        blocks[2] = jnp.where(lane == line + offset, 1.0, 0.0)
        scale = jnp.ones((GROUP, LANES), jnp.float32)
        for sub in range(0, GROUP, STEP):
            cols = columns_of(blocks[home], offset + sub, GROUP)
            for j in range(STEP):
                row = sub + j
                over = 1.0 / cols[j][row : row + 1]
                scale = jnp.where(line == row, over, scale)
                factor = jnp.where(line == row, 0.0, cols[j] * over)
                for l in range(j + 1, STEP):
                    cols[l] = cols[l] - factor * cols[l][row : row + 1]
                for q in blocks:
                    blocks[q] = blocks[q] - factor * blocks[q][row : row + 1]
        inside = jnp.logical_and(lane >= offset, lane < offset + GROUP)
        blocks = {q: blocks[q] * scale for q in blocks}
        blocks[home] = jnp.where(inside, blocks[2], blocks[home])
        for q in range(2):
            pad[offset : offset + GROUP, LANES * q : LANES * (q + 1)] = blocks[q]
        mine = square[:, LANES * home : LANES * (home + 1)]
        inside_all = jnp.logical_and(lane_all >= offset, lane_all < offset + GROUP)
        change = dot(jnp.where(inside_all, mine, 0.0), pad[...])
        square[:, LANES * home : LANES * (home + 1)] = jnp.where(inside_all, 0.0, mine)
        square[...] -= change
        square[base : base + GROUP, :] = pad[offset : offset + GROUP, :]
        pad[offset : offset + GROUP, :] = jnp.zeros((GROUP, NB), jnp.float32)
        yield base // GROUP


def ones_at(shape, begin, here_too):
    rows = lax.broadcasted_iota(jnp.int32, shape, 0) + begin
    cols = lax.broadcasted_iota(jnp.int32, shape, 1)
    return jnp.where(jnp.logical_and(rows == cols, here_too), 1.0, 0.0)


def vmem(*shape):
    return jax.ShapeDtypeStruct(shape, jnp.float32)


def scratch(*shape):
    return pltpu.VMEM(shape, jnp.float32)


def dma(n):
    return pltpu.SemaphoreType.DMA((n,))


OUTS = {
    "update": (2 * NB, NB), "vectors": (2 * NB, NB), "vectors_cols": (4 * NB, NB),
    "scaled_cols": (8, 4, SLICE, NB), "upper": (NB, NB),
}
BUFFERS = {
    "whole": (PIECE, PIECE, 2 * NB), "slab": (2 * NB, NB), "own": (SLICE, NB),
    "gram_x": (NX, PIECE, NB), "gram_y": (NY, PIECE, NB), "gram": (PIECE, PIECE, NB), "top": (PIECE, PIECE, NB),
    "columns": (8, 4, SLICE, NB), "pair": (2 * SLICE, NB), "corner": (SLICE, NB), "corner_here": (SLICE, NB),
    "terms": (8, 4, SLICE, NB), "early": (2, 4, SLICE, NB), "late": (2, 8, SLICE, NB),
    "kept": (8, SLICE, NB), "arrivals": (NY, SLICE, NB),
    "work": (NB, 2 * NB), "inverse": (NB, NB), "transform": (NB, NB), "pad": (LANES, NB),
    "inner": (NZ, 2, PIECE, NB), "inner_other": (NZ, PIECE, NB), "inner_arrivals": (NZ, PIECE, NB),
    "sum_x": (NX, PIECE, NB), "sum_y": (NY, PIECE, NB), "coupling": (PIECE, PIECE, NB),
    "scaled_own": (SLICE, NB), "scaled": (PIECE, SLICE, NB),
}
LINE = [NZ] * 4
TOTAL = [NX, NX, NY, NY] + LINE
SPREAD = [NY, NY, 6, 6]
SEMS = {
    "line": LINE, "gram": TOTAL, "tops": LINE, "top": [NX + NY, 2], "corner": [NZ + 1, 2],
    "swap_panel": [2], "swap_corner": [2], "swap_scaled": [2], "columns": SPREAD, "plane": [6, 6, NY, NY],
    "core": [2], "inner": [NZ, NZ], "coupling": TOTAL, "scaled_cols": SPREAD, "scaled": LINE,
}


def panel_kernel(piece, square, *refs):
    names = list(OUTS) + list(BUFFERS)
    b = dict(zip(names, refs))
    sems, rest = {}, list(refs[len(names) :])
    for name, counts in SEMS.items():
        sems[name], rest = rest[: len(counts)], rest[len(counts) :]

    here = Place()
    line = Line(here, lambda c: b["whole"].at[c], *sems["line"])
    total = Total(here, b["gram_x"], b["gram_y"], b["gram"], sems["gram"])
    tops = Line(here, lambda c: b["top"].at[c], *sems["tops"])
    columns = Spread(here, b["columns"], *sems["columns"])
    plane = PlaneSum(
        here, b["terms"], b["early"], b["late"], b["kept"], b["arrivals"], *sems["plane"]
    )
    coupling = Total(here, b["sum_x"], b["sum_y"], b["coupling"], sems["coupling"])
    scaled_cols = Spread(here, b["scaled_cols"], *sems["scaled_cols"])
    scaled_line = Line(here, lambda c: b["scaled"].at[c], *sems["scaled"])
    place = lambda row: (place_of(row // NX), row % NX)
    swap_panel = Swap(
        here, b["own"], lambda row, col: b["columns"].at[place(row)], sems["swap_panel"][0]
    )
    swap_corner = Swap(
        here, b["corner"], lambda row, col: b["corner_here"], sems["swap_corner"][0]
    )
    swap_scaled = Swap(
        here, b["scaled_own"], lambda row, col: b["scaled"].at[col], sems["swap_scaled"][0]
    )
    here.greet()

    b["whole"][here.col] = piece[...]
    line.start()
    corner_send, corner_recv = sems["corner"]

    def corner_copy(z, index):
        return remote(
            square.at[pl.ds(2 * SLICE * z, 2 * SLICE), pl.ds(0, NB)], b["pair"],
            corner_send.at[index], corner_recv.at[0], (here.row, 2 * z),
        )

    def corner_hand():
        return remote(
            b["pair"].at[pl.ds(SLICE, SLICE), :], b["corner"],
            corner_send.at[NZ], corner_recv.at[1], here.sibling,
        )

    @pl.when(here.col == 0)
    def _():
        for z in range(1, NZ):
            corner_copy(z, z).start()
        b["pair"][...] = square[pl.ds(0, 2 * SLICE), pl.ds(0, NB)]

    line.finish()
    slab = b["slab"]
    slab[...] = b["whole"][...].reshape(NB, 2 * NB).T
    b["own"][...] = slab[pl.ds(pl.multiple_of(SLICE * here.col, SLICE), SLICE), :]
    swap_panel.start()
    total.along_x(dot(piece[...], slab[...]))

    top_send, top_recv = sems["top"]

    def top_x(step):
        ref = b["top"].at[here.col]
        return remote(ref, ref, top_send.at[step], top_recv.at[0], here.at_x(step))

    def top_y(step):
        ref = b["top"].at[here.col]
        return remote(ref, ref, top_send.at[NX + step], top_recv.at[1], here.at_y(step))

    @pl.when(here.row == 0)
    def _():
        b["top"][here.col] = slab[pl.ds(pl.multiple_of(PIECE * here.col, PIECE), PIECE), :]
        for step in range(1, NX):
            top_x(step).start()

    product = dot(square[...], slab[...], ((0,), (0,)))
    b["terms"][...] = product.reshape(8, 4, SLICE, NB)
    plane.start()
    total.along_y()

    @pl.when(here.y == 0)
    def _():
        @pl.when(here.x > 0)
        def _():
            top_x(1).wait_recv()

        for step in range(1, NY):
            top_y(step).start()

    @pl.when(here.core == 0)
    def _():
        @pl.when(here.z > 0)
        def _():
            corner_copy(here.z, 0).wait_recv()

        corner_hand().start()
        b["corner"][...] = b["pair"][pl.ds(0, SLICE), :]

    @pl.when(here.core == 1)
    def _():
        corner_hand().wait_recv()

    swap_corner.start()
    plane.combine()

    @pl.when(here.y > 0)
    def _():
        top_y(1).wait_recv()

    total.along_z()
    tops.start()
    plane.along_y()
    swap_panel.wait_recv()
    total.finish()
    tops.finish()

    share = None
    for step in cholesky_panels(b["gram"][...].reshape(NB, NB), b["upper"], b["inverse"], b["work"]):
        if step == 1:
            share = plane.finish()
            columns.along_y()
    swap_corner.wait_recv()
    inverse = b["inverse"]
    product = dot(share, inverse[...], ((1,), (1,))) + b["corner_here"][...]
    mine = b["columns"][place(here.row)]
    vectors_here = dot(mine, inverse[...], ((1,), (1,)))
    vectors_here = vectors_here + ones_at(
        (SLICE, NB), SLICE * here.row, jnp.logical_and(here.col == 0, here.row < NB // SLICE)
    )
    b["inner"][...] = dot(vectors_here, product, ((0,), (0,))).reshape(NZ, 2, PIECE, NB)
    core = remote(
        b["inner"].at[:, 1 - here.core], b["inner_other"], sems["core"][0].at[0], sems["core"][0].at[1], here.sibling
    )
    core.start()
    inner_send, inner_recv = sems["inner"]

    def inner_copy(step):
        return remote(
            b["inner_other"].at[(here.z + step) % NZ], b["inner_arrivals"].at[step],
            inner_send.at[step], inner_recv.at[step], here.at_z(step),
        )

    transform = b["transform"]
    transform[...] = dot(inverse[...], b["top"][...].reshape(NB, NB), ((1,), (1,))) + ones_at(
        (NB, NB), 0, True
    )
    for step in inverse_panels(transform, b["pad"]):
        if step == 1:
            core.wait_recv()
            b["inner_other"][...] = b["inner_other"][...] + b["inner"][:, here.core]
            for hop in (4, 3, 5, 2, 6, 1, 7):
                inner_copy(hop).start()
        if step == 2:
            columns.along_x()
        if step == 5:
            value = b["inner_other"][here.z]
            for hop in (1, 7, 2, 6, 3, 5, 4):
                inner_copy(hop).wait_recv()
                value = value + b["inner_arrivals"][hop]
            coupling.along_x(value)
            columns.forward()
    scaled = dot(product, transform[...])
    b["scaled_own"][...] = scaled
    b["scaled_cols"][place(here.row)] = scaled
    swap_scaled.start()
    scaled_cols.along_y()
    coupling.along_y()
    b["vectors"][...] = dot(slab[...], inverse[...], ((1,), (1,))) + ones_at(
        (2 * NB, NB), 0, here.row == 0
    )
    swap_scaled.wait_recv()
    scaled_line.start()
    columns.finish()
    b["vectors_cols"][...] = dot(
        b["columns"][...].reshape(4 * NB, NB), inverse[...], ((1,), (1,))
    ) + ones_at((4 * NB, NB), 0, here.col == 0)
    coupling.along_z()
    scaled_cols.along_x()
    scaled_line.finish()
    coupling.finish()
    middle = dot(b["coupling"][...].reshape(NB, NB), transform[...])
    middle = dot(transform[...], middle, ((0,), (0,)))
    scaled_cols.forward()
    b["update"][...] = b["scaled"][...].reshape(2 * NB, NB) - dot(b["vectors"][...], middle)
    scaled_cols.finish()

    core.wait_send()
    for hop in range(1, NZ):
        inner_copy(hop).wait_send()

    @pl.when(here.col == 0)
    def _():
        for z in range(1, NZ):
            corner_copy(z, z).wait_send()

    @pl.when(here.core == 0)
    def _():
        corner_hand().wait_send()

    @pl.when(here.row == 0)
    def _():
        for step in range(1, NX):
            top_x(step).wait_send()

    @pl.when(here.y == 0)
    def _():
        for step in range(1, NY):
            top_y(step).wait_send()

    for sent in (
        line, total, tops, columns, plane, coupling, scaled_cols, scaled_line, swap_panel, swap_corner, swap_scaled
    ):
        sent.wait_send()


def per_device(panel, matrix):
    square = matrix.reshape(2 * NB, 4 * NB)
    piece = panel.reshape(2 * NB, PIECE).T
    whole = pl.BlockSpec(memory_space=pltpu.VMEM)
    update, vectors, vectors_cols, scaled_cols, upper = pl.pallas_call(
        panel_kernel,
        out_shape=[vmem(*shape) for shape in OUTS.values()],
        in_specs=[whole] * 2,
        out_specs=[whole] * len(OUTS),
        scratch_shapes=[scratch(*shape) for shape in BUFFERS.values()]
        + [dma(n) for counts in SEMS.values() for n in counts],
        compiler_params=pltpu.CompilerParams(
            collective_id=0, has_side_effects=True, vmem_limit_bytes=VMEM_LIMIT
        ),
        name="panel",
    )(piece, square)
    left = jnp.concatenate([update, vectors], axis=1)
    right = jnp.concatenate([vectors_cols, scaled_cols.reshape(4 * NB, NB)], axis=1)
    updated = square - dot(left, right, ((1,), (1,)))
    return (updated.reshape(matrix.shape), upper)


def solution(mesh):
    in_specs = (P(None, "row", "col"), P(None, "row", None, "col"))
    out_specs = (P(None, "row", None, "col"), P())
    return jax.shard_map(
        per_device, mesh=mesh, in_specs=in_specs, out_specs=out_specs, check_vma=False
    )
```

```python
import types

import jax
import jax.numpy as jnp
from jax import lax
from jax.experimental import pallas as pl
from jax.experimental.pallas import tpu as pltpu
from jax.sharding import PartitionSpec as P

MESH = pl.DeviceIdType.MESH
precise = lax.Precision.HIGHEST
NX, NY, NZ = 4, 8, 8
NB = 256
PIECE = 16
SLICE = 32
ROWS = 128
VMEM_LIMIT = 40 * 1024 * 1024


def dot(left, right, contract=((1,), (0,))):
    return lax.dot_general(
        left, right, (contract, ((), ())), preferred_element_type=jnp.float32, precision=precise
    )


def remote(src, dst, send, recv, device):
    return pltpu.make_async_remote_copy(
        src_ref=src, dst_ref=dst, send_sem=send, recv_sem=recv, device_id=device, device_id_type=MESH
    )


class Place:
    def __init__(self):
        self.row = lax.axis_index("row")
        self.col = lax.axis_index("col")
        self.y, self.x = self.row // NX, self.row % NX
        self.z, self.core = self.col // 2, self.col % 2
        self.sibling = (self.row, 2 * self.z + 1 - self.core)
        self.half, self.turn = self.row // 16, self.row % 16
        self.partner = (16 * self.half + self.col, self.turn)
        self.alone = self.turn == self.col

    def at_x(self, step):
        return (NX * self.y + (self.x + step) % NX, self.col)

    def at_y(self, step):
        return (NX * ((self.y + step) % NY) + self.x, self.col)

    def at_z(self, step):
        return (self.row, 2 * ((self.z + step) % NZ) + self.core)

    def greet(self):
        barrier = pltpu.get_barrier_semaphore()
        devices = [self.at_x(s) for s in range(1, NX)]
        devices += [self.at_y(s) for s in range(1, NY)]
        devices += [self.at_z(s) for s in range(1, NZ)]
        devices += [self.sibling]
        for device in devices:
            pl.semaphore_signal(barrier, inc=1, device_id=device, device_id_type=MESH)

        @pl.when(jnp.logical_not(self.alone))
        def _():
            pl.semaphore_signal(barrier, inc=1, device_id=self.partner, device_id_type=MESH)
            pl.semaphore_wait(barrier, len(devices) + 1)

        @pl.when(self.alone)
        def _():
            pl.semaphore_wait(barrier, len(devices))


class Ring:
    def __init__(self, count, me, device, slot, send, recv):
        self.count, self.me, self.device, self.slot = count, me, device, slot
        self.send, self.recv = send, recv

    def copy(self, step, arriving):
        owner = (self.me - step) % self.count if arriving else self.me
        ref = self.slot(owner)
        return remote(ref, ref, self.send.at[step], self.recv.at[step], self.device(step))

    def start(self):
        for step in sorted(range(1, self.count), key=lambda s: -min(s, self.count - s)):
            self.copy(step, False).start()

    def order(self):
        return sorted(range(1, self.count), key=lambda s: min(s, self.count - s))

    def wait_recv(self):
        for step in self.order():
            self.copy(step, True).wait_recv()

    def wait_send(self):
        for step in range(1, self.count):
            self.copy(step, False).wait_send()


class Line(Ring):
    def __init__(self, here, slot, send, recv, pass_send, pass_recv):
        super().__init__(NZ, here.z, here.at_z, lambda z: slot(2 * z + here.core), send, recv)
        self.here, self.across = here, lambda z: slot(2 * z + 1 - here.core)
        self.pass_send, self.pass_recv = pass_send, pass_recv

    def hand(self, step, arriving):
        owner = (self.me - step) % self.count
        ref = self.across(owner) if arriving else self.slot(owner)
        return remote(ref, ref, self.pass_send.at[step], self.pass_recv.at[step], self.here.sibling)

    def start(self):
        super().start()
        self.hand(0, False).start()

    def finish(self):
        for step in self.order():
            self.copy(step, True).wait_recv()
            self.hand(step, False).start()
        for step in [0] + self.order():
            self.hand(step, True).wait_recv()

    def wait_send(self):
        super().wait_send()
        for step in range(self.count):
            self.hand(step, False).wait_send()


def place_of(y):
    return 4 * ((y % 4) // 2) + 2 * (y // 4) + y % 2


class Spread:
    def __init__(self, here, buffer, y_send, y_recv, x_send, x_recv):
        self.here, self.buffer = here, buffer
        self.ring = Ring(
            NY, here.y, here.at_y, lambda y: buffer.at[place_of(y), here.x], y_send, y_recv
        )
        self.x_send, self.x_recv = x_send, x_recv

    def along_y(self):
        self.ring.start()

    def x_copy(self, index, arriving):
        here = self.here
        part = (0, 1, 1, 0, 0, 1)[index]
        step = (1, 1, -1, -1, 1, -1)[index]
        owner = here.x if index < 4 else (here.x - step) % NX
        if arriving:
            owner = (owner - step) % NX
        ref = self.buffer.at[pl.ds(4 * part, 4), owner]
        return remote(ref, ref, self.x_send.at[index], self.x_recv.at[index], here.at_x(step))

    def along_x(self):
        self.ring.wait_recv()
        for index in (0, 2, 1, 3):
            self.x_copy(index, False).start()

    def forward(self):
        for first, then in ((0, 4), (2, 5)):
            self.x_copy(first, True).wait_recv()
            self.x_copy(then, False).start()

    def finish(self):
        for index in (1, 3, 4, 5):
            self.x_copy(index, True).wait_recv()

    def wait_send(self):
        self.ring.wait_send()
        for index in range(6):
            self.x_copy(index, False).wait_send()


class Swap:
    def __init__(self, here, source, target_at, sems):
        self.here, self.source, self.target_at, self.sems = here, source, target_at, sems

    def copy(self, arriving):
        here = self.here
        target = self.target_at(*((here.row, here.col) if arriving else here.partner))
        return remote(self.source, target, self.sems.at[0], self.sems.at[1], here.partner)

    def start(self):
        @pl.when(jnp.logical_not(self.here.alone))
        def _():
            self.copy(False).start()

        @pl.when(self.here.alone)
        def _():
            self.target_at(self.here.row, self.here.col)[...] = self.source[...]

    def wait_recv(self):
        @pl.when(jnp.logical_not(self.here.alone))
        def _():
            self.copy(True).wait_recv()

    def wait_send(self):
        @pl.when(jnp.logical_not(self.here.alone))
        def _():
            self.copy(False).wait_send()


class Total:
    def __init__(self, here, over_x, over_y, whole, sems):
        self.here, self.over_x, self.over_y, self.whole = here, over_x, over_y, whole
        x_send, x_recv, y_send, y_recv, z_send, z_recv, p_send, p_recv = sems
        self.xs = Ring(NX, here.x, here.at_x, lambda x: over_x.at[x], x_send, x_recv)
        self.ys = Ring(NY, here.y, here.at_y, lambda y: over_y.at[y], y_send, y_recv)
        self.zs = Line(here, lambda c: whole.at[c], z_send, z_recv, p_send, p_recv)

    def along_x(self, value):
        self.over_x[self.here.x] = value
        self.xs.start()

    def along_y(self):
        self.xs.wait_recv()
        value = (self.over_x[0] + self.over_x[1]) + (self.over_x[2] + self.over_x[3])
        self.over_y[self.here.y] = value
        self.ys.start()

    def along_z(self):
        self.ys.wait_recv()
        parts = [self.over_y[y] for y in range(NY)]
        while len(parts) > 1:
            parts = [a + b for a, b in zip(parts[::2], parts[1::2])]
        self.whole[self.here.col] = parts[0]
        self.zs.start()

    def finish(self):
        self.zs.finish()

    def wait_send(self):
        self.xs.wait_send()
        self.ys.wait_send()
        self.zs.wait_send()


class PlaneSum:
    def __init__(self, here, terms, early, late, kept, arrivals, x_send, x_recv, y_send, y_recv):
        self.here, self.terms, self.early, self.late = here, terms, early, late
        self.kept, self.arrivals = kept, arrivals
        self.x_send, self.x_recv, self.y_send, self.y_recv = x_send, x_recv, y_send, y_recv

    def x_copy(self, index):
        here, way = self.here, index % 2
        step = 1 - 2 * way
        half = (way, 1 - way, way)[index // 2]
        owner = (here.x + (2 if index < 2 else step)) % NX
        source = self.terms.at[pl.ds(4 * half, 4), owner]
        target = self.early.at[way] if index < 2 else self.late.at[way, pl.ds(4 * half, 4)]
        return remote(source, target, self.x_send.at[index], self.x_recv.at[index], here.at_x(step))

    def start(self):
        for index in range(4):
            self.x_copy(index).start()

    def combine(self):
        for way in range(2):
            self.x_copy(way).wait_recv()
            owner = (self.here.x + 1 - 2 * way) % NX
            self.terms[pl.ds(4 * way, 4), owner] = self.terms[pl.ds(4 * way, 4), owner] + self.early[way]
            self.x_copy(4 + way).start()

    def y_copy(self, step):
        return remote(
            self.kept.at[place_of((self.here.y + step) % NY)], self.arrivals.at[step],
            self.y_send.at[step], self.y_recv.at[step], self.here.at_y(step),
        )

    def along_y(self):
        for index in range(2, 6):
            self.x_copy(index).wait_recv()
        self.kept[...] = self.terms[:, self.here.x] + (self.late[0] + self.late[1])
        for step in (4, 3, 5, 2, 6, 1, 7):
            self.y_copy(step).start()

    def finish(self):
        value = self.kept[place_of(self.here.y)]
        for step in (1, 7, 2, 6, 3, 5, 4):
            self.y_copy(step).wait_recv()
            value = value + self.arrivals[step]
        return value

    def wait_send(self):
        for index in range(6):
            self.x_copy(index).wait_send()
        for step in range(1, NY):
            self.y_copy(step).wait_send()


LANES, GROUP, STEP = 128, 32, 8


def columns_of(block, begin, rows):
    return [jnp.broadcast_to(block[:, begin + l : begin + l + 1], (rows, LANES)) for l in range(STEP)]


def cholesky_panels(gram, upper, inverse, work):
    line = lax.broadcasted_iota(jnp.int32, (GROUP, LANES), 0)
    rows_all = lax.broadcasted_iota(jnp.int32, (NB, NB), 0)
    cols_all = lax.broadcasted_iota(jnp.int32, (NB, NB), 1)
    work[:, :NB] = gram
    work[:, NB:] = jnp.where(rows_all == cols_all, 1.0, 0.0)
    for base in range(0, NB, GROUP):
        first, last = base // LANES, 2 + base // LANES + 1
        blocks = {q: work[base : base + GROUP, LANES * q : LANES * (q + 1)] for q in range(first, last)}
        for sub in range(0, GROUP, STEP):
            count = GROUP - sub
            number = line[:count]
            cols = columns_of(blocks[first], (base + sub) % LANES, count)
            scale = jnp.ones((STEP, LANES), jnp.float32)
            for j in range(STEP):
                pivot = cols[j][j : j + 1]
                over = 1.0 / pivot
                scale = jnp.where(number[:STEP] == j, lax.rsqrt(pivot), scale)
                factor = jnp.where(number > j, cols[j] * over, 0.0)
                for l in range(j + 1, STEP):
                    cols[l] = cols[l] - factor * cols[l][j : j + 1]
                for q in blocks:
                    blocks[q] = blocks[q] - factor * blocks[q][j : j + 1]
            for q in blocks:
                work[base + sub : base + sub + STEP, LANES * q : LANES * (q + 1)] = blocks[q][:STEP] * scale
                blocks[q] = blocks[q][STEP:]
        after = base + GROUP
        if after < NB:
            start = after // LANES
            left = work[base:after, LANES * start : NB]
            right = work[base:after, LANES * start : LANES * last]
            change = dot(left, right, ((0,), (0,)))
            work[after:, LANES * start : LANES * last] -= change[after - LANES * start :]
        else:
            upper[...] = jnp.where(rows_all <= cols_all, work[:, :NB], 0.0)
            inverse[...] = work[:, NB:]
        yield base // GROUP


def inverse_panels(square, pad):
    lane = lax.broadcasted_iota(jnp.int32, (GROUP, LANES), 1)
    line = lax.broadcasted_iota(jnp.int32, (GROUP, LANES), 0)
    pad[...] = jnp.zeros_like(pad)
    lane_all = lax.broadcasted_iota(jnp.int32, (NB, LANES), 1)
    for base in range(0, NB, GROUP):
        home, offset = base // LANES, base % LANES
        blocks = {q: square[base : base + GROUP, LANES * q : LANES * (q + 1)] for q in range(2)}
        blocks[2] = jnp.where(lane == line + offset, 1.0, 0.0)
        scale = jnp.ones((GROUP, LANES), jnp.float32)
        for sub in range(0, GROUP, STEP):
            cols = columns_of(blocks[home], offset + sub, GROUP)
            for j in range(STEP):
                row = sub + j
                over = 1.0 / cols[j][row : row + 1]
                scale = jnp.where(line == row, over, scale)
                factor = jnp.where(line == row, 0.0, cols[j] * over)
                for l in range(j + 1, STEP):
                    cols[l] = cols[l] - factor * cols[l][row : row + 1]
                for q in blocks:
                    blocks[q] = blocks[q] - factor * blocks[q][row : row + 1]
        inside = jnp.logical_and(lane >= offset, lane < offset + GROUP)
        blocks = {q: blocks[q] * scale for q in blocks}
        blocks[home] = jnp.where(inside, blocks[2], blocks[home])
        for q in range(2):
            pad[offset : offset + GROUP, LANES * q : LANES * (q + 1)] = blocks[q]
        mine = square[:, LANES * home : LANES * (home + 1)]
        inside_all = jnp.logical_and(lane_all >= offset, lane_all < offset + GROUP)
        change = dot(jnp.where(inside_all, mine, 0.0), pad[...])
        square[:, LANES * home : LANES * (home + 1)] = jnp.where(inside_all, 0.0, mine)
        square[...] -= change
        square[base : base + GROUP, :] = pad[offset : offset + GROUP, :]
        pad[offset : offset + GROUP, :] = jnp.zeros((GROUP, NB), jnp.float32)
        yield base // GROUP


def ones_at(shape, begin, here_too):
    rows = lax.broadcasted_iota(jnp.int32, shape, 0) + begin
    cols = lax.broadcasted_iota(jnp.int32, shape, 1)
    return jnp.where(jnp.logical_and(rows == cols, here_too), 1.0, 0.0)


def vmem(*shape):
    return jax.ShapeDtypeStruct(shape, jnp.float32)


def scratch(*shape):
    return pltpu.VMEM(shape, jnp.float32)


def dma(n):
    return pltpu.SemaphoreType.DMA((n,))


OUTS = dict(
    update=(2 * NB, NB), turned=(2 * NB, NB), vectors_cols=(4 * NB, NB),
    product_cols=(8, 4, SLICE, NB), upper=(NB, NB),
)
BUFFERS = dict(
    square=(2 * NB, 4 * NB), whole=(PIECE, PIECE, 2 * NB), slab=(2 * NB, NB), own=(SLICE, NB),
    gram_x=(NX, PIECE, NB), gram_y=(NY, PIECE, NB), gram=(PIECE, PIECE, NB), top=(PIECE, PIECE, NB),
    columns=(8, 4, SLICE, NB), pair=(2 * SLICE, NB), corner=(SLICE, NB), corner_here=(SLICE, NB),
    terms=(8, 4, SLICE, NB), early=(2, 4, SLICE, NB), late=(2, 8, SLICE, NB),
    kept=(8, SLICE, NB), arrivals=(NY, SLICE, NB),
    work=(NB, 2 * NB), inverse=(NB, NB), transform=(NB, NB), pad=(LANES, NB),
    inner=(NZ, 2, PIECE, NB), inner_other=(NZ, PIECE, NB), inner_arrivals=(NZ, PIECE, NB),
    sum_x=(NX, PIECE, NB), sum_y=(NY, PIECE, NB), coupling=(PIECE, PIECE, NB),
    share=(SLICE, NB), product_own=(SLICE, NB), product=(PIECE, SLICE, NB), vectors=(2 * NB, NB),
    crown_own=(2, 2, PIECE, NB), crown_pair=(2, 2, PIECE, NB), crown=(PIECE, 2, PIECE, NB),
)
LINE = [NZ] * 4
TOTAL = [NX, NX, NY, NY] + LINE
SPREAD = [NY, NY, 6, 6]
SEMS = dict(
    line=LINE, gram=TOTAL, tops=LINE, top=[NX + NY, 2], corner=[NZ + 1, 2],
    swap_panel=[2], swap_corner=[2], swap_product=[2], columns=SPREAD, plane=[6, 6, NY, NY],
    core=[2], inner=[NZ, NZ], coupling=TOTAL, product_cols=SPREAD, product=LINE,
    crown_in=[2, 2], crown_out=[NX + NY, 2], crown=LINE,
)


def panel_kernel(piece, matrix, *refs):
    names = list(OUTS) + list(BUFFERS)
    b = types.SimpleNamespace(**dict(zip(names, refs)))
    sems, rest = types.SimpleNamespace(), list(refs[len(names) :])
    for name, counts in SEMS.items():
        setattr(sems, name, rest[: len(counts)])
        rest = rest[len(counts) :]

    here = Place()
    line = Line(here, lambda c: b.whole.at[c], *sems.line)
    total = Total(here, b.gram_x, b.gram_y, b.gram, sems.gram)
    tops = Line(here, lambda c: b.top.at[c], *sems.tops)
    columns = Spread(here, b.columns, *sems.columns)
    plane = PlaneSum(
        here, b.terms, b.early, b.late, b.kept, b.arrivals, *sems.plane
    )
    coupling = Total(here, b.sum_x, b.sum_y, b.coupling, sems.coupling)
    product_cols = Spread(here, b.product_cols, *sems.product_cols)
    product_line = Line(here, lambda c: b.product.at[c], *sems.product)
    crown_line = Line(here, lambda c: b.crown.at[c], *sems.crown)
    place = lambda row: (place_of(row // NX), row % NX)
    swap_panel = Swap(
        here, b.own, lambda row, col: b.columns.at[place(row)], sems.swap_panel[0]
    )
    swap_corner = Swap(
        here, b.corner, lambda row, col: b.corner_here, sems.swap_corner[0]
    )
    swap_product = Swap(
        here, b.product_own, lambda row, col: b.product.at[col], sems.swap_product[0]
    )
    here.greet()

    b.whole[here.col] = piece[...]
    line.start()
    square = b.square
    square[:, :NB] = matrix[:, 0, :]
    corner_send, corner_recv = sems.corner

    def corner_copy(z, index):
        return remote(
            square.at[pl.ds(2 * SLICE * z, 2 * SLICE), pl.ds(0, NB)], b.pair,
            corner_send.at[index], corner_recv.at[0], (here.row, 2 * z),
        )

    def corner_hand():
        return remote(
            b.pair.at[pl.ds(SLICE, SLICE), :], b.corner,
            corner_send.at[NZ], corner_recv.at[1], here.sibling,
        )

    @pl.when(here.col == 0)
    def _():
        for z in range(1, NZ):
            corner_copy(z, z).start()
        b.pair[...] = square[pl.ds(0, 2 * SLICE), pl.ds(0, NB)]

    for d in range(1, 4):
        square[:, NB * d : NB * (d + 1)] = matrix[:, d, :]
    line.finish()
    slab = b.slab
    slab[...] = b.whole[...].reshape(NB, 2 * NB).T
    total.along_x(dot(piece[...], slab[...]))

    top_send, top_recv = sems.top

    def top_x(step):
        ref = b.top.at[here.col]
        return remote(ref, ref, top_send.at[step], top_recv.at[0], here.at_x(step))

    def top_y(step):
        ref = b.top.at[here.col]
        return remote(ref, ref, top_send.at[NX + step], top_recv.at[1], here.at_y(step))

    @pl.when(here.row == 0)
    def _():
        b.top[here.col] = slab[pl.ds(pl.multiple_of(PIECE * here.col, PIECE), PIECE), :]
        for step in range(1, NX):
            top_x(step).start()

    b.own[...] = slab[pl.ds(pl.multiple_of(SLICE * here.col, SLICE), SLICE), :]
    swap_panel.start()

    def term(half):
        value = dot(square[:, 2 * NB * half : 2 * NB * (half + 1)], slab[...], ((0,), (0,)))
        b.terms[4 * half : 4 * half + 4] = value.reshape(4, 4, SLICE, NB)

    term(0)
    total.along_y()

    @pl.when(here.y == 0)
    def _():
        @pl.when(here.x > 0)
        def _():
            top_x(1).wait_recv()

        for step in range(1, NY):
            top_y(step).start()

    term(1)
    plane.start()

    @pl.when(here.core == 0)
    def _():
        @pl.when(here.z > 0)
        def _():
            corner_copy(here.z, 0).wait_recv()

        corner_hand().start()
        b.corner[...] = b.pair[pl.ds(0, SLICE), :]

    @pl.when(here.core == 1)
    def _():
        corner_hand().wait_recv()

    swap_corner.start()

    @pl.when(here.y > 0)
    def _():
        top_y(1).wait_recv()

    tops.start()
    total.along_z()
    plane.combine()
    swap_panel.wait_recv()
    plane.along_y()
    total.finish()
    tops.finish()

    crown_in_send, crown_in_recv = sems.crown_in
    crown_send, crown_recv = sems.crown_out
    source = here.row == here.z
    level = here.y == here.z // NX

    def crown_move():
        return remote(
            b.crown_own, b.crown_pair, crown_in_send.at[0], crown_in_recv.at[0], (here.row, 2 * here.row)
        )

    def crown_hand():
        return remote(
            b.crown_pair.at[:, 1], b.crown.at[2 * here.z + 1],
            crown_in_send.at[1], crown_in_recv.at[1], here.sibling,
        )

    def crown_x(step):
        ref = b.crown.at[here.col]
        return remote(ref, ref, crown_send.at[step], crown_recv.at[0], here.at_x(step))

    def crown_y(step):
        ref = b.crown.at[here.col]
        return remote(ref, ref, crown_send.at[NX + step], crown_recv.at[1], here.at_y(step))

    def crown_first():
        @pl.when(jnp.logical_and(here.col == 0, here.row < NZ))
        def _():
            b.crown_own[0] = b.share[...].reshape(2, PIECE, NB)
            b.crown_own[1] = b.corner_here[...].reshape(2, PIECE, NB)

            @pl.when(here.row > 0)
            def _():
                crown_move().start()

            @pl.when(here.row == 0)
            def _():
                b.crown_pair[...] = b.crown_own[...]

    def crown_second():
        @pl.when(jnp.logical_and(source, here.core == 0))
        def _():
            @pl.when(here.z > 0)
            def _():
                crown_move().wait_recv()

            crown_hand().start()
            b.crown[here.col] = b.crown_pair[:, 0]

    def crown_third():
        @pl.when(source)
        def _():
            @pl.when(here.core == 1)
            def _():
                crown_hand().wait_recv()

            for step in range(1, NX):
                crown_x(step).start()

    def crown_fourth():
        @pl.when(level)
        def _():
            @pl.when(jnp.logical_not(source))
            def _():
                crown_x(1).wait_recv()

            for step in range(1, NY):
                crown_y(step).start()

    def crown_fifth():
        @pl.when(jnp.logical_not(level))
        def _():
            crown_y(1).wait_recv()

        crown_line.start()

    core = remote(
        b.inner.at[:, 1 - here.core], b.inner_other, sems.core[0].at[0], sems.core[0].at[1], here.sibling
    )
    inner_send, inner_recv = sems.inner

    def inner_copy(step):
        return remote(
            b.inner_other.at[(here.z + step) % NZ], b.inner_arrivals.at[step],
            inner_send.at[step], inner_recv.at[step], here.at_z(step),
        )

    for step in cholesky_panels(b.gram[...].reshape(NB, NB), b.upper, b.inverse, b.work):
        if step == 1:
            b.share[...] = plane.finish()
            inner = dot(b.columns[place(here.row)], b.share[...], ((0,), (0,)))
            b.inner[...] = inner.reshape(NZ, 2, PIECE, NB)
            core.start()
            swap_corner.wait_recv()
            crown_first()
            columns.along_y()
        if step == 3:
            core.wait_recv()
            b.inner_other[...] = b.inner_other[...] + b.inner[:, here.core]
            for hop in (4, 3, 5, 2, 6, 1, 7):
                inner_copy(hop).start()
        if step == 4:
            crown_second()
        if step == 6:
            crown_third()
    inverse, transform = b.inverse, b.transform
    own = dot(b.share[...], inverse[...], ((1,), (1,))) + b.corner_here[...]
    b.product_own[...] = own
    b.product_cols[place(here.row)] = own
    product_cols.along_y()
    swap_product.start()
    transform[...] = dot(inverse[...], b.top[...].reshape(NB, NB), ((1,), (1,))) + ones_at(
        (NB, NB), 0, True
    )
    value = b.inner_other[here.z]
    for hop in (1, 7, 2, 6, 3, 5, 4):
        inner_copy(hop).wait_recv()
        value = value + b.inner_arrivals[hop]
    coupling.along_x(value)
    for step in inverse_panels(transform, b.pad):
        if step == 0:
            crown_fourth()
        if step == 2:
            coupling.along_y()
        if step == 3:
            columns.along_x()
        if step == 4:
            crown_fifth()
            swap_product.wait_recv()
            product_line.start()
        if step == 6:
            columns.forward()
        if step == 7:
            coupling.along_z()
    product_cols.along_x()
    b.vectors[...] = dot(slab[...], inverse[...], ((1,), (1,))) + ones_at(
        (2 * NB, NB), 0, here.row == 0
    )
    b.turned[...] = dot(b.vectors[...], transform[...], ((1,), (1,)))
    columns.finish()
    b.vectors_cols[...] = dot(
        b.columns[...].reshape(4 * NB, NB), inverse[...], ((1,), (1,))
    ) + ones_at((4 * NB, NB), 0, here.col == 0)
    product_cols.forward()
    crown_line.finish()
    product_line.finish()
    scaled = dot(b.product[...].reshape(2 * NB, NB), transform[...])
    edge = dot(b.crown[:, 0].reshape(NB, NB), inverse[...], ((1,), (1,)))
    edge = edge + edge.T + b.crown[:, 1].reshape(NB, NB)
    coupling.finish()
    middle = dot(inverse[...], b.coupling[...].reshape(NB, NB))
    middle = dot(middle, inverse[...], ((1,), (1,))) + edge
    middle = dot(transform[...], dot(middle, transform[...]), ((0,), (0,)))
    b.update[...] = scaled - dot(b.vectors[...], middle)
    product_cols.finish()

    core.wait_send()
    for hop in range(1, NZ):
        inner_copy(hop).wait_send()

    @pl.when(here.col == 0)
    def _():
        for z in range(1, NZ):
            corner_copy(z, z).wait_send()

    @pl.when(here.core == 0)
    def _():
        corner_hand().wait_send()

    @pl.when(here.row == 0)
    def _():
        for step in range(1, NX):
            top_x(step).wait_send()

    @pl.when(here.y == 0)
    def _():
        for step in range(1, NY):
            top_y(step).wait_send()

    @pl.when(jnp.logical_and(here.col == 0, jnp.logical_and(here.row > 0, here.row < NZ)))
    def _():
        crown_move().wait_send()

    @pl.when(source)
    def _():
        @pl.when(here.core == 0)
        def _():
            crown_hand().wait_send()

        for step in range(1, NX):
            crown_x(step).wait_send()

    @pl.when(level)
    def _():
        for step in range(1, NY):
            crown_y(step).wait_send()

    for sent in (
        line, total, tops, columns, plane, coupling, product_cols, product_line, crown_line,
        swap_panel, swap_corner, swap_product,
    ):
        sent.wait_send()


def split(value):
    high = value.astype(jnp.bfloat16)
    return high, (value - high.astype(jnp.float32)).astype(jnp.bfloat16)


def update_kernel(update, turned, vectors_cols, product_cols, matrix, updated, high, low):
    @pl.when(pl.program_id(0) == 0)
    def _():
        for k, ref in enumerate((vectors_cols, product_cols)):
            high[k], low[k] = split(ref[...])

    change = None
    for k, ref in enumerate((update, turned)):
        left_high, left_low = split(ref[...])
        for left, right in ((left_high, low), (left_low, high), (left_high, high)):
            term = lax.dot_general(
                left, right[k], (((1,), (1,)), ((), ())), preferred_element_type=jnp.float32
            )
            change = term if change is None else change + term
    for d in range(4):
        updated[:, d, :] = matrix[:, d, :] - change[:, NB * d : NB * (d + 1)]


def per_device(panel, matrix):
    blocks = matrix.reshape(2 * NB, 4, NB)
    piece = panel.reshape(2 * NB, PIECE).T
    whole = pl.BlockSpec(memory_space=pltpu.VMEM)
    update, turned, vectors_cols, product_cols, upper = pl.pallas_call(
        panel_kernel,
        out_shape=[vmem(*shape) for shape in OUTS.values()],
        in_specs=[whole] * 2,
        out_specs=[whole] * len(OUTS),
        scratch_shapes=[scratch(*shape) for shape in BUFFERS.values()]
        + [dma(n) for counts in SEMS.values() for n in counts],
        compiler_params=pltpu.CompilerParams(
            collective_id=0, has_side_effects=True, vmem_limit_bytes=VMEM_LIMIT
        ),
        name="panel",
    )(piece, blocks)
    rows = pl.BlockSpec((ROWS, NB), lambda i: (i, 0))
    cols = pl.BlockSpec((4 * NB, NB), lambda i: (0, 0))
    tile = pl.BlockSpec((ROWS, 4, NB), lambda i: (i, 0, 0))
    updated = pl.pallas_call(
        update_kernel,
        grid=(2 * NB // ROWS,),
        out_shape=vmem(2 * NB, 4, NB),
        in_specs=[rows, rows, cols, cols, tile],
        out_specs=tile,
        scratch_shapes=[pltpu.VMEM((2, 4 * NB, NB), jnp.bfloat16) for _ in range(2)],
        compiler_params=pltpu.CompilerParams(vmem_limit_bytes=VMEM_LIMIT),
        name="update",
    )(update, turned, vectors_cols, product_cols.reshape(4 * NB, NB), blocks)
    return (updated.reshape(matrix.shape), upper)


def solution(mesh):
    in_specs = (P(None, "row", "col"), P(None, "row", None, "col"))
    out_specs = (P(None, "row", None, "col"), P())
    return jax.shard_map(
        per_device, mesh=mesh, in_specs=in_specs, out_specs=out_specs, check_vma=False
    )
```
